32 devices in a mesh: dp: 16 (over z, y, core), ctx: 2 (over x).
Axes of the slice: x: 2, y: 2, z: 4, core: 2. Of those that a mesh axis runs over, the one named last changes fastest.
Arguments:
- q_feat: bfloat16 [4096, 4096], P('ctx', 'dp'), may hold values from -6 to 6
- k_feat: bfloat16 [4096, 4096], P('ctx', 'dp'), may hold values from -6 to 6
- v_feat: bfloat16 [4096, 4096], P('ctx', 'dp'), may hold values from -6 to 6
- short_taps: float32 [3, 4096], P(None, 'dp'), may hold values from -3 to 3
- skip_bias: float32 [4096], P('dp'), may hold values from -4 to 4
- freqs: float32 [32], replicated, may hold values from 1 to 2048
- phases: float32 [32], replicated, may hold values from -3.140625 to 3.140625
- w_first: float32 [32, 64], replicated, may hold values from -1 to 1
- b_first: float32 [64], replicated, may hold values from -4 to 4
- w_second: float32 [64, 64], replicated, may hold values from -0.75 to 0.75
- b_second: float32 [64], replicated, may hold values from -4 to 4
- w_out: float32 [64, 256], P(None, 'dp'), may hold values from -0.0234375 to 0.0234375
- rates: float32 [256], P('dp'), may hold values from 0.1 to 2
Outputs:
- gated_out: bfloat16 [4096, 4096], P('ctx', 'dp')
The draws below stay inside these ranges and needn't reach their ends.
All inputs are finite; a program needn't handle non-finite values.
Results may differ from the reference program's by a relative error of at most 0.0061.
Values may be sent and summed in bfloat16 or wider, within the bound.
No kernel may reach another device: no remote copies, remote signals or barrier semaphores. Data moves between devices by JAX's collectives and lax.ppermute only.
A program may use at most 64 MiB of HBM per device.

```python
import math
import jax
import jax.numpy as jnp
from jax import lax

G = 256
GS = 16
D = 4096
EMB = 32
H = 64
BLK = 1024
SEQ = 4096


def level_of(rng, extent, split, smallest, largest):
    loudness = 1.0
    for dim, shards_of in split:
        heights = jax.random.uniform(jax.random.fold_in(jax.random.fold_in(rng, 6), dim), (shards_of,), jnp.float32, smallest / len(split), largest / len(split))
        loudness = loudness * jnp.repeat(jnp.exp(heights), extent[dim] // shards_of).reshape((-1,) + (1,) * (len(extent) - 1 - dim))
    return loudness


def bell_draw(key, shape, scale, most, cuts=(), kind=jnp.bfloat16):
    values = scale * jax.random.normal(key, shape, jnp.float32)
    if cuts:
        values = values * level_of(key, shape, cuts, -0.22, 0.18)
    return jnp.clip(values, -most, most).astype(kind)


def setup_inputs(seed: int = 0) -> dict:
    key_of = jax.random.split(jax.random.key(seed), 14)
    q_feat = bell_draw(key_of[0], (SEQ, D), 1.0, 6.0, ((0, 2), (1, 16)))
    k_feat = bell_draw(key_of[1], (SEQ, D), 1.0, 6.0, ((0, 2), (1, 16)))
    v_feat = bell_draw(key_of[2], (SEQ, D), 1.0, 6.0, ((0, 2), (1, 16)))
    short_taps = bell_draw(key_of[3], (3, D), 0.6, 3.0, ((1, 16),), jnp.float32)
    skip_bias = bell_draw(key_of[4], (D,), 1.0, 4.0, ((0, 16),), jnp.float32)
    freqs = jnp.clip(jnp.exp(jax.random.uniform(key_of[5], (EMB,), jnp.float32, math.log(1.0), math.log(2048.0))), 1.0, 2048.0)
    phases = jnp.clip(jax.random.uniform(key_of[6], (EMB,), jnp.float32, -3.140625, 3.140625), -3.140625, 3.140625)
    w_first = bell_draw(key_of[7], (EMB, H), EMB ** -0.5, 1.0, (), jnp.float32)
    b_first = bell_draw(key_of[8], (H,), 1.0, 4.0, (), jnp.float32)
    w_second = bell_draw(key_of[9], (H, H), H ** -0.5, 0.75, (), jnp.float32)
    b_second = bell_draw(key_of[10], (H,), 1.0, 4.0, (), jnp.float32)
    w_out = bell_draw(key_of[11], (H, G), (H * SEQ // 4) ** -0.5, 0.0234375, ((1, 16),), jnp.float32)
    rates = jnp.clip(jnp.exp(math.log(2.0) - 2.9957323 * jax.random.uniform(key_of[12], (G,), jnp.float32) ** level_of(key_of[12], (G,), ((0, 16),), -0.2, 0.2)), 0.1, 2.0)
    return {"q_feat": q_feat, "k_feat": k_feat, "v_feat": v_feat, "short_taps": short_taps, "skip_bias": skip_bias, "freqs": freqs, "phases": phases, "w_first": w_first, "b_first": b_first, "w_second": w_second, "b_second": b_second, "w_out": w_out, "rates": rates}


MAXIMUM_ACCURACY = lax.Precision.HIGHEST


def angle_table(row_count, col_count, offset, block_len):
    row_ids = jnp.arange(row_count, dtype=jnp.int32)[:, None] + offset
    col_ids = jnp.arange(col_count, dtype=jnp.int32)[None, :]
    return (math.pi / block_len) * ((row_ids * col_ids) % (2 * block_len)).astype(jnp.float32)


def forward_tables(block_len, col_count):
    angles = angle_table(block_len, col_count, 0, block_len)
    first_row = jnp.arange(block_len, dtype=jnp.int32)[:, None] == 0
    alternate = (1 - 2 * (jnp.arange(col_count, dtype=jnp.int32) % 2)).astype(jnp.float32)[None, :]
    return jnp.cos(angles), jnp.where(first_row, alternate, -jnp.sin(angles))


def inverse_tables(block_len):
    angles = angle_table(block_len, block_len, block_len, block_len)
    first_col = jnp.arange(block_len, dtype=jnp.int32)[None, :] == 0
    alternate = (1 - 2 * ((block_len + jnp.arange(block_len, dtype=jnp.int32)) % 2)).astype(jnp.float32)[:, None]
    real_part = jnp.where(first_col, 0.5 / block_len, jnp.cos(angles) / block_len)
    imag_part = jnp.where(first_col, alternate * (0.5 / block_len), -jnp.sin(angles) / block_len)
    return real_part, imag_part


def hidden_layers(positions, seq_len, freqs, phases, w_first, b_first, w_second, b_second):
    scaled = positions[:, None] / seq_len
    feature = jnp.sin(2.0 * math.pi * freqs[None, :] * scaled + phases[None, :])
    first_layer = jnp.sin(jnp.dot(feature, w_first, precision=MAXIMUM_ACCURACY) + b_first)
    return jnp.sin(jnp.dot(first_layer, w_second, precision=MAXIMUM_ACCURACY) + b_second)


def filter_rows(second, seq_len, w_cols, rate_cols):
    positions = jnp.arange(seq_len, dtype=jnp.int32).astype(jnp.float32)
    values = jnp.einsum("ph,hg->gp", second, w_cols, precision=MAXIMUM_ACCURACY)
    return values * jnp.exp(-rate_cols[:, None] * (positions[None, :] / seq_len))


def lag_spectra(filter_table, block_len, block_count):
    wide_re, wide_im = forward_tables(block_len, 2 * block_len)
    wide_re = wide_re.astype(jnp.bfloat16).astype(jnp.float32)
    wide_im = wide_im.astype(jnp.bfloat16).astype(jnp.float32)
    col_count = filter_table.shape[0]
    rounded = filter_table.astype(jnp.bfloat16).astype(jnp.float32)
    padded = jnp.concatenate([jnp.zeros((col_count, block_len), jnp.float32), rounded], 1)
    padded = padded.reshape(col_count, block_count + 1, block_len)
    spec_real = jnp.einsum("km,gjm->jgk", wide_re[:, :block_len], padded[:, :-1], precision=MAXIMUM_ACCURACY)
    spec_real = spec_real + jnp.einsum("km,gjm->jgk", wide_re[:, block_len:], padded[:, 1:], precision=MAXIMUM_ACCURACY)
    spec_imag = jnp.einsum("km,gjm->jgk", wide_im[:, :block_len], padded[:, :-1], precision=MAXIMUM_ACCURACY)
    spec_imag = spec_imag + jnp.einsum("km,gjm->jgk", wide_im[:, block_len:], padded[:, 1:], precision=MAXIMUM_ACCURACY)
    return spec_real, spec_imag


def expand(blocks, group_size):
    return jnp.repeat(jnp.swapaxes(blocks, -1, -2), group_size, axis=-1)


def accumulate(totals, pieces, filters, live_rows):
    total_re, total_im = totals
    part_re = pieces[0].astype(jnp.float32)
    part_im = pieces[1].astype(jnp.float32)
    filter_re, filter_im = filters
    total_re = total_re + (part_re * filter_re - live_rows * (part_im * filter_im))
    total_im = total_im + (live_rows * (part_re * filter_im + part_im * filter_re) + (1.0 - live_rows) * (part_im * filter_im))
    return total_re, total_im


def reference(q_feat, k_feat, v_feat, short_taps, skip_bias, freqs, phases, w_first, b_first, w_second, b_second, w_out, rates):
    block_len = BLK
    block_count = SEQ // BLK
    channels = D
    positions = jnp.arange(SEQ, dtype=jnp.int32).astype(jnp.float32)
    second = hidden_layers(positions, SEQ, freqs, phases, w_first, b_first, w_second, b_second)
    filter_table = filter_rows(second, SEQ, w_out, rates)
    spec_re, spec_im = lag_spectra(filter_table, block_len, block_count)
    narrow = forward_tables(block_len, block_len)
    twiddle_real = narrow[0].astype(jnp.bfloat16)
    twiddle_imaginary = narrow[1].astype(jnp.bfloat16)
    back = inverse_tables(block_len)
    inverse_real = back[0].astype(jnp.bfloat16)
    inverse_imaginary = back[1].astype(jnp.bfloat16)
    live_rows = (jnp.arange(block_len, dtype=jnp.int32) >= 1).astype(jnp.float32)[:, None]

    extended = jnp.concatenate([jnp.zeros((2, channels), jnp.float32), v_feat.astype(jnp.float32)], 0)
    smoothed = short_taps[0] * extended[2:] + short_taps[1] * extended[1:-1] + short_taps[2] * extended[:-2]
    signal = (k_feat.astype(jnp.float32) * smoothed).astype(jnp.bfloat16)
    block_pieces = signal.reshape(block_count, block_len, channels).astype(jnp.float32)
    input_real = jnp.einsum("rl,jlq->jrq", twiddle_real.astype(jnp.float32), block_pieces, precision=MAXIMUM_ACCURACY).astype(jnp.bfloat16)
    input_imaginary = jnp.einsum("rl,jlq->jrq", twiddle_imaginary.astype(jnp.float32), block_pieces, precision=MAXIMUM_ACCURACY).astype(jnp.bfloat16)
    pieces = []
    for target in range(block_count):
        totals = (jnp.zeros((block_len, channels), jnp.float32), jnp.zeros((block_len, channels), jnp.float32))
        for lag_index in range(target + 1):
            filters = (expand(spec_re[lag_index], GS), expand(spec_im[lag_index], GS))
            totals = accumulate(totals, (input_real[target - lag_index], input_imaginary[target - lag_index]), filters, live_rows)
        conv_block = jnp.dot(inverse_real, totals[0].astype(jnp.bfloat16), preferred_element_type=jnp.float32)
        conv_block = conv_block + jnp.dot(inverse_imaginary, totals[1].astype(jnp.bfloat16), preferred_element_type=jnp.float32)
        pieces.append(conv_block)
    conv = jnp.concatenate(pieces, 0)
    return (q_feat.astype(jnp.float32) * (conv + skip_bias * signal.astype(jnp.float32))).astype(jnp.bfloat16)
```

```python
import functools
import math

import jax
import jax.numpy as jnp
import ml_dtypes
import numpy as np
from jax import lax
from jax.experimental import pallas as pl
from jax.experimental.pallas import tpu as pltpu
from jax.sharding import PartitionSpec as P

BLK = 1024
LANES = 128
PACK = 4
EDGE = 16
MIB = 1 << 20

BF16 = jnp.bfloat16
F32 = jnp.float32
EXACT = lax.Precision.HIGHEST

SINE = (6.283185159611166, -41.341654929345026, 81.60099819273452, -76.54965682347806, 39.53581373236733)


def transform_tables(block_len):
    rows = np.arange(block_len)[:, None]
    cols = np.arange(block_len)[None, :]
    angles = np.pi / block_len * ((rows * cols) % (2 * block_len))
    imag = -np.sin(angles)
    imag[0] = 1 - 2 * (np.arange(block_len) % 2)
    forward = np.concatenate([np.cos(angles), imag], 0)
    turned = np.pi / block_len * (((rows + block_len) * cols) % (2 * block_len))
    back_re = np.cos(turned) / block_len
    back_im = -np.sin(turned) / block_len
    back_re[:, 0] = 0.5 / block_len
    back_im[:, 0] = (1 - 2 * ((block_len + np.arange(block_len)) % 2)) * (0.5 / block_len)
    inverse = np.concatenate([back_re, back_im], 1)
    return forward.astype(ml_dtypes.bfloat16), inverse.astype(ml_dtypes.bfloat16)


def dot32(a, b):
    return jnp.dot(a, b, preferred_element_type=F32)


def iota(shape, dim):
    return lax.broadcasted_iota(jnp.int32, shape, dim)


def sine_of_quarter(w):
    z = w * w
    total = jnp.full_like(z, SINE[-1])
    for c in SINE[-2::-1]:
        total = total * z + c
    return w * total


def cos_turns(t):
    u = t - jnp.round(t)
    return sine_of_quarter(0.25 - jnp.abs(u))


def two_parts(x):
    high = x.astype(BF16)
    return high, (x - high.astype(F32)).astype(BF16)


def dot_parts(a, w):
    a_high, a_low = two_parts(a)
    return dot32(a_high, w[0]) + dot32(a_low, w[0]) + dot32(a_high, w[1])


def shifted(v, before):
    row = iota((8, v.shape[1]), 0)
    last = before[EDGE - 1 : EDGE]
    last_but_one = before[EDGE - 2 : EDGE - 1]
    one = pltpu.roll(v, 1, 0)
    two = pltpu.roll(v, 2, 0)
    one_head = jnp.where(row == 0, last, one[:8])
    two_head = jnp.where(row == 0, last_but_one, jnp.where(row == 1, last, two[:8]))
    one = jnp.concatenate([one_head, one[8:]], 0)
    two = jnp.concatenate([two_head, two[8:]], 0)
    return one, two


def mix(v, before, k, taps):
    one, two = shifted(v, before)
    mixed = taps[0:1] * v + taps[1:2] * one + taps[2:3] * two
    return (k * mixed).astype(BF16)


def signal_kernel(v_ref, prev_ref, k_ref, rim_ref, taps_ref, edge_ref, *sig_refs):
    first = jnp.logical_and(pl.program_id(0) == 0, pl.program_id(1) == 0)
    before = jnp.where(first, rim_ref[...].astype(F32), prev_ref[...].astype(F32))
    v = v_ref[...]
    sig = mix(v.astype(F32), before, k_ref[...].astype(F32), taps_ref[...])
    for h, ref in enumerate(sig_refs):
        ref[...] = sig[:, h * LANES : (h + 1) * LANES]
    edge_ref[...] = v[v.shape[0] - EDGE :]


def make_signal(v, k, rim, taps, halves):
    span, channels = v.shape
    blocks = span // BLK
    step = BLK // 2
    parts = BLK // step
    at = lambda b, r: (b * parts + r, 0)
    before = lambda b, r: (jnp.maximum((b * parts + r) * (step // EDGE) - 1, 0), 0)
    return pl.pallas_call(
        signal_kernel,
        grid=(blocks, parts),
        in_specs=[
            pl.BlockSpec((step, channels), at),
            pl.BlockSpec((EDGE, channels), before),
            pl.BlockSpec((step, channels), at),
            pl.BlockSpec((EDGE, channels), lambda b, r: (0, 0)),
            pl.BlockSpec((3, channels), lambda b, r: (0, 0)),
        ],
        out_specs=[pl.BlockSpec((EDGE, channels), lambda b, r: (0, 0))]
        + [pl.BlockSpec((step, LANES), lambda b, r: (r, b))] * halves,
        out_shape=[jax.ShapeDtypeStruct((EDGE, channels), BF16)]
        + [jax.ShapeDtypeStruct((BLK, blocks * LANES), BF16)] * halves,
        compiler_params=pltpu.CompilerParams(vmem_limit_bytes=16 * MIB),
        cost_estimate=pl.CostEstimate(flops=8 * span * channels, bytes_accessed=6 * span * channels, transcendentals=0),
    )(v, v, k, rim, taps)


def patch_head(sig_ref, own_ref, v_ref, k_ref, rim_ref, taps_ref):
    own_ref[...] = sig_ref[...]
    head = mix(v_ref[...].astype(F32), rim_ref[...].astype(F32), k_ref[...].astype(F32), taps_ref[...])
    own_ref[0:EDGE, 0:LANES] = head


def transform(fwd, source, out, index=None):
    step = BLK // 2

    @pl.loop(0, 2 * BLK // step)
    def _(i):
        rows = pl.ds(pl.multiple_of(i * step, step), step)
        value = dot32(fwd[rows, :], source).astype(BF16)
        if index is None:
            out[rows, :] = value
        else:
            out[index, rows, :] = value


def group_picker(lags, half, groups, group_size, lag_count):
    wide = lag_count * groups
    shape = (4 * wide, LANES)
    row = iota(shape, 0) % (2 * wide)
    group = (half * LANES + iota(shape, 1)) // group_size
    pieces = []
    for j in lags:
        low = jnp.logical_and(row < wide, row == (j - 1) * groups + group)
        high = row - wide == j * groups + group
        pieces.append(jnp.logical_or(low, high).astype(F32).astype(BF16))
    return jnp.concatenate(pieces, 1)


def pair_lists(spans, span_blocks):
    return [
        [
            (s, b, s * span_blocks + c - b)
            for s in spans
            for b in range(span_blocks)
            if s * span_blocks + c - b >= 0
        ]
        for c in range(span_blocks)
    ]


def multiply_spectra(x_of, spec, picker, lags, pair_sets, y_refs):
    step = LANES

    def chunk(start, head):
        rows = pl.ds(start, step)
        lower = pl.ds(start + BLK, step)
        h_re = dot32(spec[rows, :], picker)
        h_im = dot32(spec[lower, :], picker)
        if head:
            top = iota(h_re.shape, 0) == 0
            h_cross = jnp.where(top, 0.0, h_im)
            h_last = jnp.where(top, h_im, h_re)
        else:
            h_cross = h_im
            h_last = h_re
        x_cache = {}
        for pairs, y_ref in zip(pair_sets, y_refs):
            for c, listed in enumerate(pairs):
                lanes = slice(c * LANES, (c + 1) * LANES)
                y_re = None
                y_im = None
                for s, b, j in listed:
                    if (s, b) not in x_cache:
                        x_cache[(s, b)] = (x_of(s, rows, b).astype(F32), x_of(s, lower, b).astype(F32))
                    x_re, x_im = x_cache[(s, b)]
                    at = lags.index(j) * LANES
                    here = slice(at, at + LANES)
                    re = x_re * h_re[:, here] - x_im * h_cross[:, here]
                    im = x_re * h_cross[:, here] + x_im * h_last[:, here]
                    y_re = re if y_re is None else y_re + re
                    y_im = im if y_im is None else y_im + im
                y_ref[rows, lanes] = y_re.astype(BF16)
                y_ref[lower, lanes] = y_im.astype(BF16)

    chunk(0, True)

    @pl.loop(1, BLK // step)
    def _(i):
        chunk(pl.multiple_of(i * step, step), False)


def filter_spectra(
    freqs, phases, w_first, b_first, w_second, b_second, w_out, rates, fwd_copy, fwd, filt, spec, lag_count, seq_len
):
    emb = freqs.shape[1]
    hidden = w_second.shape[0]
    groups = rates.shape[1]
    wide = lag_count * groups
    turn = 1.0 / (2.0 * math.pi)

    def repeat_lanes(value, times):
        return jnp.concatenate([value] * times, 1)

    def diagonal(value):
        rows, cols = value.shape
        tiled = jnp.concatenate([repeat_lanes(value, PACK)] * PACK, 0)
        keep = iota(tiled.shape, 0) // rows == iota(tiled.shape, 1) // cols
        return jnp.where(keep, tiled, 0.0)

    first_w = two_parts(diagonal(w_first[...] * turn))
    second_w = two_parts(diagonal(w_second[...] * turn))
    first_b = repeat_lanes(b_first[...] * turn - 0.25, PACK)
    second_b = repeat_lanes(b_second[...] * turn - 0.25, PACK)
    spread = (iota((groups, 2 * wide), 1) % groups == iota((groups, 2 * wide), 0)).astype(F32)
    out_cols = jnp.dot(w_out[...], spread, precision=EXACT, preferred_element_type=F32)
    out_rows = jnp.concatenate([out_cols] * PACK, 0)
    lag_of = (iota((PACK * hidden, 2 * wide), 1) % wide) // groups
    slot_of = iota((PACK * hidden, 2 * wide), 0) // hidden
    out_w = [
        two_parts(jnp.where(lag_of == q * PACK + slot_of, out_rows, 0.0)) for q in range(lag_count // PACK)
    ]
    rate = jnp.dot(
        jnp.broadcast_to(rates[...], (8, groups)), spread, precision=EXACT, preferred_element_type=F32
    )[0:1]

    fine = 32
    freq = repeat_lanes(freqs[...], PACK)
    phase = repeat_lanes(phases[...], PACK) * turn
    scaled = freq * 4097.0
    freq_high = scaled - (scaled - freq)
    freq_low = freq - freq_high
    lanes = PACK * emb
    slot = iota((BLK // fine, lanes), 1) // emb
    coarse = iota((BLK // fine, lanes), 0)
    fine_at = iota((fine, lanes), 0).astype(F32)

    def turns(at, scale):
        high = freq_high * at * scale
        return (high - jnp.round(high)) + freq_low * at * scale

    fine_turns = turns(fine_at, 1.0 / seq_len)
    fine_cos = cos_turns(fine_turns)
    fine_sin = cos_turns(fine_turns - 0.25)
    coarse_parts = []
    for q in range(lag_count // PACK):
        at = ((q * PACK + slot) * (BLK // fine) + coarse).astype(F32)
        angle = turns(at, fine / seq_len) + phase
        coarse_parts.append((cos_turns(angle), cos_turns(angle - 0.25)))

    step = 256
    for i in range(BLK // step):
        total = None
        for q in range(lag_count // PACK):
            coarse_cos, coarse_sin = coarse_parts[q]
            pieces = []
            for a in range(i * step // fine, (i + 1) * step // fine):
                pieces.append(coarse_sin[a : a + 1] * fine_cos + coarse_cos[a : a + 1] * fine_sin)
            feature = jnp.concatenate(pieces, 0)
            first = cos_turns(dot_parts(feature, first_w) + first_b)
            second = cos_turns(dot_parts(first, second_w) + second_b)
            part = dot_parts(second, out_w[q])
            total = part if total is None else total + part
        lag = (iota((step, 2 * wide), 1) % wide) // groups
        position = (lag * BLK + iota((step, 2 * wide), 0) + i * step).astype(F32)
        decay = jnp.exp(-rate * (position * (1.0 / seq_len)))
        filt[i * step : (i + 1) * step, :] = (total * decay).astype(BF16)

    fwd_copy.wait()
    step = BLK // 2

    @pl.loop(0, 2 * BLK // step)
    def _(i):
        rows = pl.ds(pl.multiple_of(i * step, step), step)
        value = dot32(fwd[rows, :], filt[...])
        flip = jnp.logical_and(iota(value.shape, 0) % 2 == 1, iota(value.shape, 1) >= wide)
        value = jnp.where(flip, -value, value)
        high, low = two_parts(value)
        spec[rows, 0 : 2 * wide] = high
        spec[rows, 2 * wide : 4 * wide] = low


def filter_kernel(
    distances, lag_count, seq_len, half, group_size, span_blocks,
    freqs, phases, w_first, b_first, w_second, b_second, w_out, rates, fwd_hbm, *rest,
):
    groups = rates.shape[1]
    if half is None:
        spec, fwd, filt, sems = rest
    else:
        (inv_hbm, sig, v_head, k_head, rim, taps, skip, spec, own_conv, *rest) = rest
        sent = rest[: len(distances)]
        fwd, filt, inv, own, x_own, y_own, *rest = rest[len(distances) :]
        y_sent = rest[: len(distances)]
        sems = rest[len(distances)]
    fwd_copy = pltpu.make_async_copy(fwd_hbm, fwd, sems.at[0])
    fwd_copy.start()
    if half is not None:
        inv_copy = pltpu.make_async_copy(inv_hbm, inv, sems.at[1])
        inv_copy.start()
    filter_spectra(
        freqs, phases, w_first, b_first, w_second, b_second, w_out, rates, fwd_copy, fwd, filt, spec, lag_count, seq_len
    )
    if half is None:
        return
    patch_head(sig, own, v_head, k_head, rim, taps)
    transform(fwd, own[...], x_own)
    sets = [pair_lists([0], span_blocks)] + [pair_lists([s], span_blocks) for s in distances]
    lags = sorted({j for pairs in sets for listed in pairs for _, _, j in listed})
    picker = group_picker(lags, half, groups, group_size, lag_count)
    multiply_spectra(
        lambda s, rows, b: x_own[rows, b * LANES : (b + 1) * LANES], spec, picker, lags, sets, [y_own, *y_sent]
    )
    inv_copy.wait()
    step = BLK // 2

    @pl.loop(0, BLK // step)
    def _(i):
        rows = pl.ds(pl.multiple_of(i * step, step), step)
        for out, y in zip(sent, y_sent):
            out[rows, :] = dot32(inv[rows, :], y[...]).astype(BF16)
        conv = dot32(inv[rows, :], y_own[...])
        for c in range(span_blocks):
            lanes = slice(c * LANES, (c + 1) * LANES)
            own_conv[rows, lanes] = conv[:, lanes] + skip[...] * own[rows, lanes].astype(F32)


def vmem():
    return pl.BlockSpec(memory_space=pltpu.VMEM)


def anywhere():
    return pl.BlockSpec(memory_space=pl.ANY)


def half_of(rows, half):
    return pl.BlockSpec((rows, LANES), lambda i: (0, half))


def whole_of(array):
    return pl.BlockSpec(array.shape, lambda i: (0,) * array.ndim)


def run_filter(params, tables, sig, v, k, rim, taps, skip, half, distances, seq_len, span_blocks, group_size):
    forward, inverse = tables
    lag_count = seq_len // BLK
    groups = params[-1].shape[1]
    wide = lag_count * groups
    width = span_blocks * LANES
    in_specs = [whole_of(p) for p in params] + [anywhere()]
    operands = [*params, forward]
    out_shape = [jax.ShapeDtypeStruct((2 * BLK, 4 * wide), BF16)]
    scratch = [pltpu.VMEM((2 * BLK, BLK), BF16), pltpu.VMEM((BLK, 2 * wide), BF16)]
    flops = 2 * 2 * BLK * BLK * 2 * wide + 40 * seq_len * 64 * 8
    if half is not None:
        in_specs += [anywhere(), whole_of(sig)] + [half_of(EDGE, half)] * 3 + [half_of(3, half), half_of(1, half)]
        operands += [inverse, sig, v, k, rim, taps, skip]
        out_shape += [jax.ShapeDtypeStruct((BLK, width), F32)]
        out_shape += [jax.ShapeDtypeStruct((BLK, width), BF16)] * len(distances)
        scratch += [pltpu.VMEM((BLK, 2 * BLK), BF16), pltpu.VMEM((BLK, width), BF16)]
        scratch += [pltpu.VMEM((2 * BLK, width), BF16)] * (2 + len(distances))
        flops += 2 * 2 * BLK * BLK * width * (2 + len(distances))
    scratch += [pltpu.SemaphoreType.DMA((2,))]
    return pl.pallas_call(
        functools.partial(filter_kernel, distances, lag_count, seq_len, half, group_size, span_blocks),
        grid=(1,),
        in_specs=in_specs,
        out_specs=[whole_of(s) for s in out_shape],
        out_shape=out_shape,
        scratch_shapes=scratch,
        compiler_params=pltpu.CompilerParams(vmem_limit_bytes=48 * MIB),
        cost_estimate=pl.CostEstimate(flops=4 * flops, bytes_accessed=12 * MIB, transcendentals=0),
    )(*operands)


def receive_kernel(
    half, lag_count, group_size, groups, span_blocks, spans,
    spec, fwd_hbm, inv_hbm, sig, v_head, k_head, rim, taps, skip, q, *rest,
):
    came = rest[: spans - 1]
    out, fwd, inv, own, x, y, sems = rest[spans - 1 :]
    fwd_copy = pltpu.make_async_copy(fwd_hbm, fwd, sems.at[0])
    inv_copy = pltpu.make_async_copy(inv_hbm, inv, sems.at[1])
    fwd_copy.start()
    inv_copy.start()
    patch_head(sig, own, v_head, k_head, rim, taps)
    fwd_copy.wait()
    transform(fwd, own[...], x, 0)
    for s in range(1, spans):
        transform(fwd, came[s - 1][...], x, s)
    pairs = pair_lists(range(spans), span_blocks)
    lags = sorted({j for listed in pairs for _, _, j in listed})
    picker = group_picker(lags, half, groups, group_size, lag_count)
    multiply_spectra(
        lambda s, rows, b: x[s, rows, b * LANES : (b + 1) * LANES], spec, picker, lags, [pairs], [y]
    )
    inv_copy.wait()
    step = BLK // 2

    @pl.loop(0, BLK // step)
    def _(i):
        start = pl.multiple_of(i * step, step)
        rows = pl.ds(start, step)
        conv = dot32(inv[rows, :], y[...])
        for c in range(span_blocks):
            lanes = slice(c * LANES, (c + 1) * LANES)
            there = pl.ds(c * BLK + start, step)
            total = conv[:, lanes] + skip[...] * own[rows, lanes].astype(F32)
            out[there, :] = (q[there, :].astype(F32) * total).astype(BF16)


def run_receive(spec, tables, sig, v, k, rim, taps, skip, q, came, half, lag_count, groups, group_size, span_blocks):
    spans = len(came) + 1
    width = span_blocks * LANES
    rows = span_blocks * BLK
    channels = q.shape[1]
    return pl.pallas_call(
        functools.partial(receive_kernel, half, lag_count, group_size, groups, span_blocks, spans),
        grid=(1,),
        in_specs=[whole_of(spec), anywhere(), anywhere(), whole_of(sig)]
        + [half_of(EDGE, half)] * 3
        + [half_of(3, half), half_of(1, half), half_of(rows, half)]
        + [whole_of(c) for c in came],
        out_specs=half_of(rows, half),
        out_shape=jax.ShapeDtypeStruct((rows, channels), BF16),
        scratch_shapes=[
            pltpu.VMEM((2 * BLK, BLK), BF16),
            pltpu.VMEM((BLK, 2 * BLK), BF16),
            pltpu.VMEM((BLK, width), BF16),
            pltpu.VMEM((spans, 2 * BLK, width), BF16),
            pltpu.VMEM((2 * BLK, width), BF16),
            pltpu.SemaphoreType.DMA((2,)),
        ],
        compiler_params=pltpu.CompilerParams(vmem_limit_bytes=48 * MIB),
        cost_estimate=pl.CostEstimate(
            flops=4 * 2 * 2 * BLK * BLK * width * (spans + 1), bytes_accessed=12 * MIB, transcendentals=0
        ),
    )(spec, *tables, sig, v, k, rim, taps, skip, q, *came)


def last_kernel(count, out_in, own, q, *rest):
    out = rest[count]
    total = own[...]
    for came in rest[:count]:
        total = total + came[...].astype(F32)
    out[...] = (q[...].astype(F32) * total).astype(BF16)


def run_last(out, own, q, came, half, span_blocks):
    step = BLK // 2
    parts = BLK // step
    by_block = pl.BlockSpec((step, LANES), lambda c, r: (r, c))
    by_row = pl.BlockSpec((step, LANES), lambda c, r: (c * parts + r, half))
    return pl.pallas_call(
        functools.partial(last_kernel, len(came)),
        grid=(span_blocks, parts),
        in_specs=[anywhere(), by_block, by_row] + [by_block] * len(came),
        out_specs=by_row,
        out_shape=jax.ShapeDtypeStruct(out.shape, out.dtype),
        input_output_aliases={0: 0},
        compiler_params=pltpu.CompilerParams(vmem_limit_bytes=16 * MIB),
    )(out, own, q, *came)


def on_device(
    q_feat,
    k_feat,
    v_feat,
    short_taps,
    skip_bias,
    freqs,
    phases,
    w_first,
    b_first,
    w_second,
    b_second,
    w_out,
    rates,
):
    span_rows, channels = q_feat.shape
    groups = rates.shape[0]
    group_size = channels // groups
    spans = lax.axis_size("ctx")
    seq_len = span_rows * spans
    span_blocks = span_rows // BLK
    halves = channels // LANES
    lag_count = seq_len // BLK
    distances = list(range(1, spans))
    forward, inverse = transform_tables(BLK)
    tables = (jnp.asarray(forward), jnp.asarray(inverse))

    def along(value, by):
        return lax.ppermute(value, "ctx", [(i, i + by) for i in range(spans - by)])

    row = lambda value: value.reshape(1, -1)
    skip = row(skip_bias)
    params = [row(freqs), row(phases), w_first, row(b_first), w_second, row(b_second), w_out, row(rates)]

    if spans > 2:
        rim = along(v_feat[span_rows - EDGE :], 1)
        _, *sigs = make_signal(v_feat, k_feat, rim, short_taps, halves)
    else:
        nothing = jnp.zeros((EDGE, channels), BF16)
        edge, *sigs = make_signal(v_feat, k_feat, nothing, short_taps, halves)
        rim = along(edge, 1)

    by_result = halves - 1 if halves > 1 else None
    by_signal = [h for h in range(halves) if h != by_result]
    came = {h: [along(sigs[h], s) for s in distances] for h in by_signal}
    sig = None if by_result is None else sigs[by_result]
    spec, *rest = run_filter(
        params, tables, sig, v_feat, k_feat, rim, short_taps, skip, by_result, distances, seq_len, span_blocks, group_size
    )
    if by_result is not None:
        own, *sent = rest
        results = [along(value, s) for value, s in zip(sent, distances)]
    out = None
    for h in by_signal:
        out = run_receive(
            spec, tables, sigs[h], v_feat, k_feat, rim, short_taps, skip, q_feat, came[h], h, lag_count, groups,
            group_size, span_blocks,
        )
    if by_result is not None:
        out = run_last(out, own, q_feat, results, by_result, span_blocks)
    return out


def solution(mesh):
    return jax.shard_map(
        on_device,
        mesh=mesh,
        in_specs=(
            P("ctx", "dp"),
            P("ctx", "dp"),
            P("ctx", "dp"),
            P(None, "dp"),
            P("dp"),
            P(),
            P(),
            P(),
            P(),
            P(),
            P(),
            P(None, "dp"),
            P("dp"),
        ),
        out_specs=P("ctx", "dp"),
        check_vma=False,
    )
```
